512 devices in a mesh: dp: 16 (over z_lo, y), task: 32 (over z_hi, x, core).
Axes of the slice: x: 4, y: 8, z: 8 (z_hi: 4, z_lo: 2; z = z_hi * 2 + z_lo), core: 2. Of those that a mesh axis runs over, the one named last changes fastest.
Arguments:
- hidden: bfloat16 [2048, 4096], P('dp', 'task'), may hold values from -6 to 6
- proj_weight: bfloat16 [4096, 4096], P(None, 'task'), may hold values from -0.09375 to 0.09375
- task_embed: bfloat16 [8192, 512], P('task'), may hold values from -0.25 to 0.25
- event_piece: int32 [8192, 2048], P('task', 'dp'), may hold values from 0 to 7
- censored: int32 [8192, 2048], P('task', 'dp'), may hold values 0 or 1
- offset: int32 [8192, 2048], P('task', 'dp'), may hold values from 1 to 64
Outputs:
- hidden_grad: bfloat16 [4096, 2048], P('task', 'dp')
- weight_grad: bfloat16 [4096, 4096], P(None, 'task')
- embed_grad: bfloat16 [8192, 512], P('task')
The draws below stay inside these ranges and needn't reach their ends.
All inputs are finite; a program needn't handle non-finite values. No bound on the sum of `censored` on one device may be relied on, other than what follows from the above.
Results may differ from the reference program's by a relative error of at most 0.029.
Values may be sent and summed in bfloat16 or wider, within the bound.
A program may use at most 64 MiB of HBM per device.

```python
import math
import jax
import jax.numpy as jnp
from jax import lax

D = 4096
PIECES = 8
RANK = 512
SPAN = 64
TASK_DEV = 256
TASKS = 8192
ROWS = 2048
N_TASK = 32


def touch_ends(result, stream_key, smallest, largest):
    spot = [jax.random.randint(jax.random.fold_in(stream_key, axis), (), 0, length) for axis, length in enumerate(result.shape)]
    widest = result.shape.index(max(result.shape))
    neighbour = spot[:widest] + [(spot[widest] + 1) % result.shape[widest]] + spot[widest + 1:]
    return result.at[tuple(spot)].set(smallest).at[tuple(neighbour)].set(largest)


def block_scale(stream_key, extent, pieces, low, high):
    loudness, own = 1.0, jax.random.fold_in(stream_key, 6)
    for position, blocks in pieces:
        steps = jnp.exp(jax.random.uniform(jax.random.fold_in(own, position), (blocks,), jnp.float32, low / len(pieces), high / len(pieces)))
        loudness = loudness * jnp.repeat(steps, extent[position] // blocks).reshape([-1 if axis == position else 1 for axis in range(len(extent))])
    return loudness


def centred(own_key, extent, deviation, most, cuts=(), kind=jnp.bfloat16):
    entries = jax.random.normal(own_key, extent, jnp.float32) * deviation
    if len(cuts) > 0:
        entries = block_scale(own_key, extent, cuts, -0.22, 0.18) * entries
    return jnp.clip(entries, min=-most, max=most).astype(kind)


def setup_inputs(seed: int = 0) -> dict:
    key_list = jax.random.split(jax.random.key(seed), 7)
    hidden = centred(key_list[0], (ROWS, D), 1.0, 6.0, ((0, 16), (1, 32)))
    proj_weight = centred(key_list[1], (D, PIECES * RANK), D ** -0.5, 0.09375, ((1, 32),))
    task_embed = centred(key_list[2], (TASKS, RANK), RANK ** -0.5, 0.25, ((0, 32),))
    event_piece = touch_ends(jax.random.randint(key_list[3], (TASKS, ROWS), 0, PIECES), jax.random.fold_in(key_list[3], 1), 0, PIECES - 1).astype(jnp.int32)
    censored = touch_ends((jax.random.randint(key_list[4], (TASKS, ROWS), 0, 2) < 1).astype(jnp.int32), jax.random.fold_in(key_list[4], 1), 0, 1)
    offset = touch_ends(jax.random.randint(key_list[5], (TASKS, ROWS), 1, SPAN + 1), jax.random.fold_in(key_list[5], 1), 1, SPAN).astype(jnp.int32)
    return dict(hidden=hidden, proj_weight=proj_weight, task_embed=task_embed, event_piece=event_piece, censored=censored, offset=offset)


def reference(hidden, proj_weight, task_embed, event_piece, censored, offset):
    scale = 1.0 / math.sqrt(ROWS)
    proj = jnp.dot(hidden, proj_weight, preferred_element_type=jnp.float32).astype(jnp.bfloat16)
    proj_split = proj.astype(jnp.float32).reshape(ROWS, PIECES, RANK)
    piece_ids = lax.broadcasted_iota(jnp.int32, (PIECES, 1, 1), 0)

    def task_block(total, index):
        first = (index * TASK_DEV).astype(jnp.int32)
        embed_rows = lax.dynamic_slice_in_dim(task_embed, first, TASK_DEV, 0).astype(jnp.float32)
        pieces_here = lax.dynamic_slice_in_dim(event_piece, first, TASK_DEV, 0).astype(jnp.int32)
        censor_here = lax.dynamic_slice_in_dim(censored, first, TASK_DEV, 0)
        offset_here = lax.dynamic_slice_in_dim(offset, first, TASK_DEV, 0)
        logits = jnp.einsum('tk,rpk->ptr', embed_rows, proj_split)
        before = piece_ids < pieces_here[None]
        inside = piece_ids == pieces_here[None]
        exposure = jnp.where(before, jnp.float32(1.0), jnp.where(inside, offset_here[None].astype(jnp.float32) / SPAN, jnp.float32(0.0)))
        event = (1 - censor_here).astype(jnp.float32)[None]
        logit_grad = ((jnp.exp(logits) * exposure - event * inside.astype(jnp.float32)) * scale).astype(jnp.bfloat16)
        grad_wide = logit_grad.astype(jnp.float32)
        embed_block = jnp.einsum('ptr,rpk->tk', grad_wide, proj_split).astype(jnp.bfloat16)
        partial_value = jnp.einsum('ptr,tk->rpk', grad_wide, embed_rows).reshape(ROWS, PIECES * RANK)
        partial_value = lax.optimization_barrier(partial_value.astype(jnp.bfloat16)).astype(jnp.float32)
        return (total + partial_value, embed_block)
    start = jnp.zeros((ROWS, PIECES * RANK), jnp.float32)
    proj_total, embed_blocks = lax.scan(task_block, start, jnp.arange(N_TASK, dtype=jnp.int32))
    embed_grad = embed_blocks.reshape(TASKS, RANK)
    proj_grad = proj_total.astype(jnp.bfloat16)
    block_cols = PIECES * RANK // N_TASK

    def column_block(total, index):
        first = (index * block_cols).astype(jnp.int32)
        weight_cols = lax.dynamic_slice_in_dim(proj_weight, first, block_cols, 1)
        grad_cols = lax.dynamic_slice_in_dim(proj_grad, first, block_cols, 1)
        partial_value = lax.dot_general(weight_cols, grad_cols, (((1,), (1,)), ((), ())), preferred_element_type=jnp.float32)
        partial_value = lax.optimization_barrier(partial_value.astype(jnp.bfloat16)).astype(jnp.float32)
        return (total + partial_value, None)
    hidden_total, unused = lax.scan(column_block, jnp.zeros((D, ROWS), jnp.float32), jnp.arange(N_TASK, dtype=jnp.int32))
    hidden_grad = hidden_total.astype(jnp.bfloat16)
    weight_grad = lax.dot_general(hidden, proj_grad, (((0,), (0,)), ((), ())), preferred_element_type=jnp.float32).astype(jnp.bfloat16)
    return (hidden_grad, weight_grad, embed_grad)
```

```python
import functools
import math

import jax
import jax.numpy as jnp
from jax import lax
from jax.experimental import pallas as pl
from jax.experimental.pallas import tpu as pltpu
from jax.sharding import PartitionSpec as P

SPAN = 64
B = 128
NX = 4
NZ = 4
NY = 8
MESH = pl.DeviceIdType.MESH
BF = jnp.bfloat16
F32 = jnp.float32
NSEM = 224


def dot(a, b):
    return jnp.dot(a, b, preferred_element_type=F32)


def dot_nt(a, b):
    return lax.dot_general(a, b, (((1,), (1,)), ((), ())), preferred_element_type=F32)


def kernel(
    scale,
    h_ref, w_hbm, e_hbm, ep_hbm, cen_hbm, off_hbm,
    hg_ref, wg_ref, eg_ref,
    w, e, ep, cen, off, wt, et, hbuf, pbuf, lg, fy,
    part, crecv, s1, xrecv, s2, zrecv,
    hpart, hcrecv, hs1, hxrecv, hs2, hzrecv,
    pg, pgy, wown, wpeer, epart, erecv, eown, epeer,
    lsem, ssem, rsem,
):
    dp = lax.axis_index("dp")
    t = lax.axis_index("task")
    y, zl = dp % NY, dp // NY
    core, x, zh = t % 2, (t // 2) % NX, t // (2 * NX)
    mate = 1 - core

    core_dev = (dp, t + 1 - 2 * core)
    x_dev = {i: (dp, zh * 2 * NX + ((x + i) % NX) * 2 + core) for i in range(1, NX)}
    z_dev = {i: (dp, ((zh + i) % NZ) * 2 * NX + x * 2 + core) for i in range(1, NZ)}
    y_dev = {i: (zl * NY + (y + i) % NY, t) for i in range(1, NY)}
    zl_dev = ((1 - zl) * NY + y, t)
    near_y = (1, 7, 2, 6, 3, 5, 4)
    near = (1, 3, 2)

    ids = {}
    sent = []

    def send(src, dst, key, dev):
        slot = ids.setdefault(key, len(ids))
        copy = pltpu.make_async_remote_copy(
            src, dst, ssem.at[len(sent)], rsem.at[slot], device_id=dev, device_id_type=MESH
        )
        copy.start()
        sent.append(copy)

    def arrive(dst, key):
        slot = ids.setdefault(key, len(ids))
        pltpu.make_async_remote_copy(
            dst, dst, ssem.at[0], rsem.at[slot], device_id=core_dev, device_id_type=MESH
        ).wait_recv()

    loads = [
        pltpu.make_async_copy(src, dst, lsem.at[i])
        for i, (src, dst) in enumerate(
            ((w_hbm, w), (e_hbm, e), (ep_hbm, ep), (cen_hbm, cen), (off_hbm, off))
        )
    ]
    for copy in loads:
        copy.start()

    barrier = pltpu.get_barrier_semaphore()
    peers = [core_dev, zl_dev, *x_dev.values(), *z_dev.values(), *y_dev.values()]
    for dev in peers:
        pl.semaphore_signal(barrier, inc=1, device_id=dev, device_id_type=MESH)
    hbuf[t] = jnp.transpose(h_ref[...].astype(F32)).astype(BF)
    pl.semaphore_wait(barrier, len(peers))

    def block(q, i, c):
        return ((zh + q) % NZ) * 2 * NX + ((x + i) % NX) * 2 + c

    def spread(buf, name, q):
        mine = buf.at[block(q, 0, core)]
        for i in near:
            send(mine, mine, (name, "x", (NX - i) % NX, q), x_dev[i])
        send(mine, mine, (name, "c", 0, q), core_dev)

    def gather_start(buf, name):
        mine = buf.at[t]
        for q in near:
            send(mine, mine, (name, "z", (NZ - q) % NZ), z_dev[q])
        spread(buf, name, 0)

    def gather_finish(buf, name):
        def from_z(q):
            arrive(buf.at[block(q, 0, core)], (name, "z", q))
            spread(buf, name, q)

        def from_x(q):
            for i in near:
                got = buf.at[block(q, i, core)]
                arrive(got, (name, "x", i, q))
                send(got, got, (name, "c", i, q), core_dev)

        from_z(1)
        from_z(3)
        from_x(0)
        from_z(2)
        from_x(1)
        from_x(3)
        from_x(2)
        for q in (0, 1, 3, 2):
            for i in range(NX):
                arrive(buf.at[block(q, i, mate)], (name, "c", i, q))

    gather_start(hbuf, "h")
    loads[0].wait()
    loads[1].wait()
    for i in range(32):
        wt[:, i * B:(i + 1) * B] = jnp.transpose(w[i * B:(i + 1) * B, :].astype(F32)).astype(BF)
    for i in range(4):
        et[i * B:(i + 1) * B, :] = jnp.transpose(e[:, i * B:(i + 1) * B].astype(F32)).astype(BF)
    for copy in loads[2:]:
        copy.wait()
    gather_finish(hbuf, "h")

    pbuf[t] = dot(wt[...], hbuf[...].reshape(32 * B, B)).astype(BF)
    gather_start(pbuf, "p")
    for i in near_y:
        there = (y + i) % NY
        send(hbuf.at[pl.ds(there * 4, 4)], fy.at[y], ("f", NY - i), y_dev[i])
    gather_finish(pbuf, "p")

    def core_step(p, r, name, q):
        send(p.at[q, mate], r.at[q], (name, "c", q), core_dev)

    def x_step(p, r, s, xr, name, q):
        arrive(r.at[q], (name, "c", q))
        for i in (*near, 0):
            there = (x + i) % NX
            total = p[q, core, there].astype(F32) + r[q, there].astype(F32)
            s[q, i] = total.astype(BF)
            if i:
                send(s.at[q, i], xr.at[q, NX - i], (name, "x", NX - i, q), x_dev[i])

    def z_step(s, xr, s2, zr, name, q):
        total = s[q, 0].astype(F32)
        for i in near:
            arrive(xr.at[q, i], (name, "x", i, q))
            total += xr[q, i].astype(F32)
        if q:
            s2[q] = total.astype(BF)
            send(s2.at[q], zr.at[NZ - q], (name, "z", NZ - q), z_dev[q])
        return total

    def last_step(total, zr, name):
        for q in near:
            arrive(zr.at[q], (name, "z", q))
            total += zr[q].astype(F32)
        return total

    offset = off[...].astype(F32) * (1.0 / SPAN)
    event = (1 - cen[...]).astype(F32)
    piece = ep[...]

    def grads(q):
        zq = (zh + q) % NZ
        for h in range(2):
            p = zq * 2 + h
            proj = pbuf[pl.ds(p * 4, 4)].reshape(4 * B, B)
            logits = dot(e[...], proj)
            inside = piece == p
            exposure = jnp.where(piece > p, 1.0, jnp.where(inside, offset, 0.0))
            grad = (jnp.exp(logits) * exposure - jnp.where(inside, event, 0.0)) * scale
            grad = grad.astype(BF)
            lg[p] = grad
            out = dot(et[...], grad).astype(BF)
            for j in range(4):
                part[q, j % 2, 2 * h + j // 2] = out[j * B:(j + 1) * B]
        core_step(part, crecv, "g", q)

    grads(2)
    grads(1)
    x_step(part, crecv, s1, xrecv, "g", 2)
    grads(3)
    x_step(part, crecv, s1, xrecv, "g", 1)
    grads(0)
    x_step(part, crecv, s1, xrecv, "g", 3)
    x_step(part, crecv, s1, xrecv, "g", 0)

    total = jnp.zeros(e.shape, F32)
    for p in range(8):
        total += dot_nt(lg[p], pbuf[4 * p:4 * p + 4].reshape(4 * B, B))
    epart[...] = total.astype(BF).reshape(epart.shape)
    for i in near_y:
        send(epart.at[(y + i) % NY], erecv.at[NY - i], ("e", NY - i), y_dev[i])

    for q in (2, 1, 3):
        z_step(s1, xrecv, s2, zrecv, "g", q)
    total = z_step(s1, xrecv, s2, zrecv, "g", 0)
    total = last_step(total, zrecv, "g")
    grad = total.astype(BF)
    pg[...] = jnp.transpose(total).astype(BF)
    for i in near_y:
        send(pg, pgy.at[y], ("pg", NY - i), y_dev[i])

    def hidden(q):
        zq = (zh + q) % NZ
        first = pl.multiple_of(zq * 2 * NX * B, 2 * NX * B)
        out = dot(w[pl.ds(first, 2 * NX * B), :], grad).astype(BF)
        for j in range(2 * NX):
            hpart[q, j % 2, j // 2] = out[j * B:(j + 1) * B]
        core_step(hpart, hcrecv, "d", q)

    hidden(2)
    hidden(1)
    x_step(hpart, hcrecv, hs1, hxrecv, "d", 2)
    hidden(3)
    x_step(hpart, hcrecv, hs1, hxrecv, "d", 1)
    hidden(0)
    x_step(hpart, hcrecv, hs1, hxrecv, "d", 3)
    x_step(hpart, hcrecv, hs1, hxrecv, "d", 0)

    total = epart[y].astype(F32)
    for i in near_y:
        arrive(erecv.at[i], ("e", i))
        total += erecv[i].astype(F32)
    eown[...] = total.astype(BF)
    send(eown, epeer, ("ez",), zl_dev)

    for q in (2, 1, 3):
        z_step(hs1, hxrecv, hs2, hzrecv, "d", q)
    hidden_total = z_step(hs1, hxrecv, hs2, hzrecv, "d", 0)

    fy[y] = hbuf[pl.ds(y * 4, 4)]
    pgy[y] = pg[...]
    for i in near_y:
        arrive(fy.at[(y + i) % NY], ("f", i))
        arrive(pgy.at[(y + i) % NY], ("pg", i))
    total = jnp.zeros((4 * B, B), F32)
    for i in range(0, NY, 2):
        feats = jnp.concatenate([fy[i].reshape(4 * B, B), fy[i + 1].reshape(4 * B, B)], 1)
        total += dot(feats, jnp.concatenate([pgy[i], pgy[i + 1]], 0))
    wown[...] = total.astype(BF)
    send(wown, wpeer, ("wz",), zl_dev)

    arrive(epeer, ("ez",))
    eg_ref[y] = (eown[...].astype(F32) + epeer[...].astype(F32)).astype(BF)
    for i in near_y:
        send(eg_ref.at[y], eg_ref.at[y], ("ey", NY - i), y_dev[i])

    arrive(wpeer, ("wz",))
    wg_ref[y] = (wown[...].astype(F32) + wpeer[...].astype(F32)).astype(BF)
    for i in near_y:
        send(wg_ref.at[y], wg_ref.at[y], ("wy", NY - i), y_dev[i])

    hg_ref[...] = last_step(hidden_total, hzrecv, "d").astype(BF)

    for i in near_y:
        arrive(eg_ref.at[(y + i) % NY], ("ey", i))
    for i in near_y:
        arrive(wg_ref.at[(y + i) % NY], ("wy", i))
    for copy in sent:
        copy.wait_send()
    assert len(sent) <= NSEM and len(ids) <= NSEM


def shards(hidden, proj_weight, task_embed, event_piece, censored, offset):
    rows = hidden.shape[0]
    scale = 1.0 / math.sqrt(rows * lax.axis_size("dp"))
    tasks, rank = task_embed.shape
    features, cols = proj_weight.shape
    vmem = pl.BlockSpec(memory_space=pltpu.VMEM)
    hbm = pl.BlockSpec(memory_space=pl.ANY)

    def reduce_buffers():
        return [
            pltpu.VMEM((NZ, 2, NX, B, B), BF),
            pltpu.VMEM((NZ, NX, B, B), BF),
            pltpu.VMEM((NZ, NX, B, B), BF),
            pltpu.VMEM((NZ, NX, B, B), BF),
            pltpu.VMEM((NZ, B, B), BF),
            pltpu.VMEM((NZ, B, B), BF),
        ]

    hidden_grad, weight_grad, embed_grad = pl.pallas_call(
        functools.partial(kernel, scale),
        out_shape=(
            jax.ShapeDtypeStruct((B, rows), BF),
            jax.ShapeDtypeStruct((NY, features // NY, cols), BF),
            jax.ShapeDtypeStruct((NY, tasks // NY, rank), BF),
        ),
        in_specs=[vmem] + [hbm] * 5,
        out_specs=(vmem, vmem, vmem),
        scratch_shapes=[
            pltpu.VMEM((features, cols), BF),
            pltpu.VMEM((tasks, rank), BF),
            pltpu.VMEM((tasks, rows), jnp.int32),
            pltpu.VMEM((tasks, rows), jnp.int32),
            pltpu.VMEM((tasks, rows), jnp.int32),
            pltpu.VMEM((cols, features), BF),
            pltpu.VMEM((rank, tasks), BF),
            pltpu.VMEM((32, B, B), BF),
            pltpu.VMEM((32, B, B), BF),
            pltpu.VMEM((8, tasks, rows), BF),
            pltpu.VMEM((NY, 4, B, B), BF),
            *reduce_buffers(),
            *reduce_buffers(),
            pltpu.VMEM((B, B), BF),
            pltpu.VMEM((NY, B, B), BF),
            pltpu.VMEM((4 * B, B), BF),
            pltpu.VMEM((4 * B, B), BF),
            pltpu.VMEM((NY, tasks // NY, rank), BF),
            pltpu.VMEM((NY, tasks // NY, rank), BF),
            pltpu.VMEM((tasks // NY, rank), BF),
            pltpu.VMEM((tasks // NY, rank), BF),
            pltpu.SemaphoreType.DMA((5,)),
            pltpu.SemaphoreType.DMA((NSEM,)),
            pltpu.SemaphoreType.DMA((NSEM,)),
        ],
        compiler_params=pltpu.CompilerParams(
            collective_id=0, has_side_effects=True, vmem_limit_bytes=48 * 2**20
        ),
    )(hidden, proj_weight, task_embed, event_piece, censored, offset)
    return (
        hidden_grad,
        weight_grad.reshape(features, cols),
        embed_grad.reshape(tasks, rank),
    )


def solution(mesh):
    return jax.shard_map(
        shards,
        mesh=mesh,
        in_specs=(
            P("dp", "task"),
            P(None, "task"),
            P("task", None),
            P("task", "dp"),
            P("task", "dp"),
            P("task", "dp"),
        ),
        out_specs=(P("task", "dp"), P(None, "task"), P("task", None)),
        check_vma=False,
    )
```

```python
import functools
import math

import jax
import jax.numpy as jnp
from jax import lax
from jax.experimental import pallas as pl
from jax.experimental.pallas import tpu as pltpu
from jax.sharding import PartitionSpec as P

SPAN = 64
B = 128
NX = 4
NZ = 4
NY = 8
MESH = pl.DeviceIdType.MESH
BF = jnp.bfloat16
F32 = jnp.float32
NSEM = 224


def dot(a, b):
    return jnp.dot(a, b, preferred_element_type=F32)


def dot_nt(a, b):
    return lax.dot_general(a, b, (((1,), (1,)), ((), ())), preferred_element_type=F32)


def kernel(
    scale,
    h_ref, w_hbm, e_hbm, ep_hbm, cen_hbm, off_hbm,
    hg_ref, wg_ref, eg_ref,
    w, e, ep, cen, off, wt, et, hbuf, pbuf, lg, fy,
    part, crecv, s1, xrecv, s2, zrecv,
    hpart, hcrecv, hs1, hxrecv, hs2, hzrecv,
    pg, pgy, wown, wpeer, epart, erecv, eown, epeer,
    lsem, ssem, rsem,
):
    dp = lax.axis_index("dp")
    t = lax.axis_index("task")
    y, zl = dp % NY, dp // NY
    core, x, zh = t % 2, (t // 2) % NX, t // (2 * NX)
    mate = 1 - core

    core_dev = (dp, t + 1 - 2 * core)
    x_dev = {i: (dp, zh * 2 * NX + ((x + i) % NX) * 2 + core) for i in range(1, NX)}
    z_dev = {i: (dp, ((zh + i) % NZ) * 2 * NX + x * 2 + core) for i in range(1, NZ)}
    y_dev = {i: (zl * NY + (y + i) % NY, t) for i in range(1, NY)}
    zl_dev = ((1 - zl) * NY + y, t)
    near_y = (1, 7, 2, 6, 3, 5, 4)
    near = (1, 3, 2)

    ids = {}
    sent = []

    def send(src, dst, key, dev):
        slot = ids.setdefault(key, len(ids))
        copy = pltpu.make_async_remote_copy(
            src, dst, ssem.at[len(sent)], rsem.at[slot], device_id=dev, device_id_type=MESH
        )
        copy.start()
        sent.append(copy)

    def arrive(dst, key):
        slot = ids.setdefault(key, len(ids))
        pltpu.make_async_remote_copy(
            dst, dst, ssem.at[0], rsem.at[slot], device_id=core_dev, device_id_type=MESH
        ).wait_recv()

    loads = [
        pltpu.make_async_copy(src, dst, lsem.at[i])
        for i, (src, dst) in enumerate(
            ((w_hbm, w), (e_hbm, e), (ep_hbm, ep), (cen_hbm, cen), (off_hbm, off))
        )
    ]
    for copy in loads:
        copy.start()

    barrier = pltpu.get_barrier_semaphore()
    peers = [core_dev, zl_dev, *x_dev.values(), *z_dev.values(), *y_dev.values()]
    for dev in peers:
        pl.semaphore_signal(barrier, inc=1, device_id=dev, device_id_type=MESH)
    hbuf[zh, x, core] = jnp.transpose(h_ref[...].astype(F32)).astype(BF)
    pl.semaphore_wait(barrier, len(peers))

    def block(buf, q, i, c):
        return buf.at[(zh + q) % NZ, (x + i) % NX, c]

    def spread(buf, name, q):
        mine = block(buf, q, 0, core)
        for i in near:
            send(mine, mine, (name, "x", (NX - i) % NX, q), x_dev[i])
        send(mine, mine, (name, "c", 0, q), core_dev)

    def gather_start(buf, name):
        mine = block(buf, 0, 0, core)
        for q in near:
            send(mine, mine, (name, "z", (NZ - q) % NZ), z_dev[q])
        spread(buf, name, 0)

    def gather_finish(buf, name, between=lambda: None):
        def from_z(q):
            arrive(block(buf, q, 0, core), (name, "z", q))
            spread(buf, name, q)

        def from_x(q):
            for i in near:
                got = block(buf, q, i, core)
                arrive(got, (name, "x", i, q))
                send(got, got, (name, "c", i, q), core_dev)

        from_z(1)
        from_z(3)
        from_x(0)
        from_z(2)
        from_x(1)
        from_x(3)
        from_x(2)
        between()
        for q in (0, 1, 3, 2):
            for i in range(NX):
                arrive(block(buf, q, i, mate), (name, "c", i, q))

    gather_start(hbuf, "h")
    loads[0].wait()
    loads[1].wait()
    for i in range(32):
        wt[:, i * B:(i + 1) * B] = jnp.transpose(w[i * B:(i + 1) * B, :].astype(F32)).astype(BF)
    for i in range(4):
        et[i * B:(i + 1) * B, :] = jnp.transpose(e[:, i * B:(i + 1) * B].astype(F32)).astype(BF)
    for copy in loads[2:]:
        copy.wait()

    def features_to_planes():
        for i in (4, 1, 7, 2, 6, 3, 5):
            there = (y + i) % NZ
            send(hbuf.at[there, :, core], fy.at[y, :, core], ("f", NY - i), y_dev[i])

    gather_finish(hbuf, "h", features_to_planes)

    pbuf[zh, x, core] = dot(wt[...], hbuf[...].reshape(32 * B, B)).astype(BF)
    gather_start(pbuf, "p")
    gather_finish(pbuf, "p")

    def core_step(p, r, name, q):
        send(p.at[q, mate], r.at[q], (name, "c", q), core_dev)

    def x_step(p, r, s, xr, name, q):
        arrive(r.at[q], (name, "c", q))
        for i in (*near, 0):
            there = (x + i) % NX
            total = p[q, core, there].astype(F32) + r[q, there].astype(F32)
            s[q, i] = total.astype(BF)
            if i:
                send(s.at[q, i], xr.at[q, NX - i], (name, "x", NX - i, q), x_dev[i])

    def z_step(s, xr, s2, zr, name, q):
        total = s[q, 0].astype(F32)
        for i in near:
            arrive(xr.at[q, i], (name, "x", i, q))
            total += xr[q, i].astype(F32)
        if q:
            s2[q] = total.astype(BF)
            send(s2.at[q], zr.at[NZ - q], (name, "z", NZ - q), z_dev[q])
        return total

    def last_step(total, zr, name):
        for q in near:
            arrive(zr.at[q], (name, "z", q))
            total += zr[q].astype(F32)
        return total

    offset = off[...].astype(F32) * (1.0 / SPAN)
    event = (1 - cen[...]).astype(F32)
    piece = ep[...]

    def grads(q):
        zq = (zh + q) % NZ
        for h in range(2):
            p = zq * 2 + h
            proj = pbuf[zq, 2 * h:2 * h + 2].reshape(4 * B, B)
            logits = dot(e[...], proj)
            inside = piece == p
            exposure = jnp.where(piece > p, 1.0, jnp.where(inside, offset, 0.0))
            grad = (jnp.exp(logits) * exposure - jnp.where(inside, event, 0.0)) * scale
            grad = grad.astype(BF)
            lg[p] = grad
            out = dot(et[...], grad).astype(BF)
            for j in range(4):
                part[q, j % 2, 2 * h + j // 2] = out[j * B:(j + 1) * B]
        core_step(part, crecv, "g", q)

    grads(2)
    grads(1)
    x_step(part, crecv, s1, xrecv, "g", 2)
    grads(3)
    x_step(part, crecv, s1, xrecv, "g", 1)
    grads(0)
    x_step(part, crecv, s1, xrecv, "g", 3)
    x_step(part, crecv, s1, xrecv, "g", 0)

    total = jnp.zeros(e.shape, F32)
    for p in range(8):
        total += dot_nt(lg[p], pbuf[p // 2, 2 * (p % 2):2 * (p % 2) + 2].reshape(4 * B, B))
    epart[...] = total.astype(BF).reshape(epart.shape)
    for i in near_y:
        send(epart.at[(y + i) % NY], erecv.at[NY - i], ("e", NY - i), y_dev[i])

    for q in (2, 1, 3):
        z_step(s1, xrecv, s2, zrecv, "g", q)
    total = z_step(s1, xrecv, s2, zrecv, "g", 0)
    total = last_step(total, zrecv, "g")
    grad = total.astype(BF)
    pg[...] = jnp.transpose(total).astype(BF)
    for i in near_y:
        send(pg, pgy.at[y], ("pg", NY - i), y_dev[i])

    def hidden(q):
        zq = (zh + q) % NZ
        first = pl.multiple_of(zq * 2 * NX * B, 2 * NX * B)
        out = dot(w[pl.ds(first, 2 * NX * B), :], grad).astype(BF)
        for j in range(2 * NX):
            hpart[q, j % 2, j // 2] = out[j * B:(j + 1) * B]
        core_step(hpart, hcrecv, "d", q)

    hidden(2)
    hidden(1)
    x_step(hpart, hcrecv, hs1, hxrecv, "d", 2)
    hidden(3)
    x_step(hpart, hcrecv, hs1, hxrecv, "d", 1)
    hidden(0)
    x_step(hpart, hcrecv, hs1, hxrecv, "d", 3)
    x_step(hpart, hcrecv, hs1, hxrecv, "d", 0)

    total = epart[y].astype(F32)
    for i in near_y:
        arrive(erecv.at[i], ("e", i))
        total += erecv[i].astype(F32)
    eown[...] = total.astype(BF)
    send(eown, epeer, ("ez",), zl_dev)

    chunk = y % NZ
    for i in near_y:
        got = fy.at[(y + i) % NY, :, core]
        arrive(got, ("f", i))
        send(got, got, ("fc", i), core_dev)
    fy[y] = hbuf[chunk]
    pgy[y] = pg[...]

    arrive(epeer, ("ez",))
    eg_ref[y] = (eown[...].astype(F32) + epeer[...].astype(F32)).astype(BF)
    for i in near_y:
        send(eg_ref.at[y], eg_ref.at[y], ("ey", NY - i), y_dev[i])

    for i in near_y:
        arrive(fy.at[(y + i) % NY, :, mate], ("fc", i))
    for i in near_y:
        arrive(pgy.at[(y + i) % NY], ("pg", i))
    for j in range(NX):
        total = jnp.zeros((2 * B, B), F32)
        for i in range(0, NY, 2):
            feats = jnp.concatenate([fy[k, j].reshape(2 * B, B) for k in (i, i + 1)], 1)
            total += dot(feats, jnp.concatenate([pgy[i], pgy[i + 1]], 0))
        wown[j] = total.astype(BF).reshape(2, B, B)
        send(wown.at[j], wpeer.at[j], ("wz", j), zl_dev)

    for q in (2, 1, 3):
        z_step(hs1, hxrecv, hs2, hzrecv, "d", q)
    hidden_total = z_step(hs1, hxrecv, hs2, hzrecv, "d", 0)

    for j in range(NX):
        arrive(wpeer.at[j], ("wz", j))
        mine = wg_ref.at[chunk, j]
        wg_ref[chunk, j] = (wown[j].astype(F32) + wpeer[j].astype(F32)).astype(BF)
        for i in (1, 7, 2 if j < 2 else 6):
            send(mine, mine, ("wy", NY - i, j), y_dev[i])

    hg_ref[...] = last_step(hidden_total, hzrecv, "d").astype(BF)

    for i in near_y:
        arrive(eg_ref.at[(y + i) % NY], ("ey", i))
    for j in range(NX):
        for i in (1, 7, 6 if j < 2 else 2):
            arrive(wg_ref.at[(chunk + i) % NZ, j], ("wy", i, j))
    for copy in sent:
        copy.wait_send()
    assert len(sent) <= NSEM and len(ids) <= NSEM


def shards(hidden, proj_weight, task_embed, event_piece, censored, offset):
    rows = hidden.shape[0]
    scale = 1.0 / math.sqrt(rows * lax.axis_size("dp"))
    tasks, rank = task_embed.shape
    features, cols = proj_weight.shape
    vmem = pl.BlockSpec(memory_space=pltpu.VMEM)
    hbm = pl.BlockSpec(memory_space=pl.ANY)

    def reduce_buffers():
        return [
            pltpu.VMEM((NZ, 2, NX, B, B), BF),
            pltpu.VMEM((NZ, NX, B, B), BF),
            pltpu.VMEM((NZ, NX, B, B), BF),
            pltpu.VMEM((NZ, NX, B, B), BF),
            pltpu.VMEM((NZ, B, B), BF),
            pltpu.VMEM((NZ, B, B), BF),
        ]

    hidden_grad, weight_grad, embed_grad = pl.pallas_call(
        functools.partial(kernel, scale),
        out_shape=(
            jax.ShapeDtypeStruct((B, rows), BF),
            jax.ShapeDtypeStruct((NZ, NX, 2, B, cols), BF),
            jax.ShapeDtypeStruct((NY, tasks // NY, rank), BF),
        ),
        in_specs=[vmem] + [hbm] * 5,
        out_specs=(vmem, vmem, vmem),
        scratch_shapes=[
            pltpu.VMEM((features, cols), BF),
            pltpu.VMEM((tasks, rank), BF),
            pltpu.VMEM((tasks, rows), jnp.int32),
            pltpu.VMEM((tasks, rows), jnp.int32),
            pltpu.VMEM((tasks, rows), jnp.int32),
            pltpu.VMEM((cols, features), BF),
            pltpu.VMEM((rank, tasks), BF),
            pltpu.VMEM((NZ, NX, 2, B, B), BF),
            pltpu.VMEM((NZ, NX, 2, B, B), BF),
            pltpu.VMEM((8, tasks, rows), BF),
            pltpu.VMEM((NY, NX, 2, B, B), BF),
            *reduce_buffers(),
            *reduce_buffers(),
            pltpu.VMEM((B, B), BF),
            pltpu.VMEM((NY, B, B), BF),
            pltpu.VMEM((NX, 2, B, B), BF),
            pltpu.VMEM((NX, 2, B, B), BF),
            pltpu.VMEM((NY, tasks // NY, rank), BF),
            pltpu.VMEM((NY, tasks // NY, rank), BF),
            pltpu.VMEM((tasks // NY, rank), BF),
            pltpu.VMEM((tasks // NY, rank), BF),
            pltpu.SemaphoreType.DMA((5,)),
            pltpu.SemaphoreType.DMA((NSEM,)),
            pltpu.SemaphoreType.DMA((NSEM,)),
        ],
        compiler_params=pltpu.CompilerParams(
            collective_id=0, has_side_effects=True, vmem_limit_bytes=62 * 2**20
        ),
    )(hidden, proj_weight, task_embed, event_piece, censored, offset)
    return (
        hidden_grad,
        weight_grad.reshape(features, cols),
        embed_grad.reshape(tasks, rank),
    )


def solution(mesh):
    return jax.shard_map(
        shards,
        mesh=mesh,
        in_specs=(
            P("dp", "task"),
            P(None, "task"),
            P("task", None),
            P("task", "dp"),
            P("task", "dp"),
            P("task", "dp"),
        ),
        out_specs=(P("task", "dp"), P(None, "task"), P("task", None)),
        check_vma=False,
    )
```

```python
import functools
import math

import jax
import jax.numpy as jnp
from jax import lax
from jax.experimental import pallas as pl
from jax.experimental.pallas import tpu as pltpu
from jax.sharding import PartitionSpec as P

SPAN = 64
B = 128
NX = 4
NZ = 4
NY = 8
MESH = pl.DeviceIdType.MESH
BF = jnp.bfloat16
F32 = jnp.float32
NSEM = 224


def dot(a, b):
    return jnp.dot(a, b, preferred_element_type=F32)


def dot_nt(a, b):
    return lax.dot_general(a, b, (((1,), (1,)), ((), ())), preferred_element_type=F32)


def kernel(
    scale,
    h_ref, w_hbm, e_hbm, ep_hbm, cen_hbm, off_hbm,
    hg_hbm, wg_hbm, eg_hbm,
    w, e, ep, cen, off, wt, et, hbuf, pbuf, lg, fy,
    part, crecv, s1, xrecv, s2, zrecv,
    hpart, hcrecv, hs1, hxrecv, hs2, hzrecv,
    pg, pgy, wown, wpeer, epart, erecv, eown, epeer,
    hg_ref, wg_ref, eg_ref,
    lsem, osem, fsend, frecv, ssem, rsem,
):
    dp = lax.axis_index("dp")
    t = lax.axis_index("task")
    y, zl = dp % NY, dp // NY
    core, x, zh = t % 2, (t // 2) % NX, t // (2 * NX)
    mate = 1 - core

    core_dev = (dp, t + 1 - 2 * core)
    x_dev = {i: (dp, zh * 2 * NX + ((x + i) % NX) * 2 + core) for i in range(1, NX)}
    z_dev = {i: (dp, ((zh + i) % NZ) * 2 * NX + x * 2 + core) for i in range(1, NZ)}
    y_dev = {i: (zl * NY + (y + i) % NY, t) for i in range(1, NY)}
    zl_dev = ((1 - zl) * NY + y, t)
    far_y = (4, 3, 5, 2, 6, 1, 7)
    far = (1, 3, 2)

    ids = {}
    sent = []
    stored = []

    def store(src, dst):
        copy = pltpu.make_async_copy(src, dst, osem.at[len(stored)])
        copy.start()
        stored.append(copy)

    def send(src, dst, key, dev):
        slot = ids.setdefault(key, len(ids))
        copy = pltpu.make_async_remote_copy(
            src, dst, ssem.at[len(sent)], rsem.at[slot], device_id=dev, device_id_type=MESH
        )
        copy.start()
        sent.append(copy)

    def arrive(dst, key):
        slot = ids.setdefault(key, len(ids))
        pltpu.make_async_remote_copy(
            dst, dst, ssem.at[0], rsem.at[slot], device_id=core_dev, device_id_type=MESH
        ).wait_recv()

    loads = [
        pltpu.make_async_copy(src, dst, lsem.at[i])
        for i, (src, dst) in enumerate(
            ((w_hbm, w), (e_hbm, e), (ep_hbm, ep), (cen_hbm, cen), (off_hbm, off))
        )
    ]
    for copy in loads:
        copy.start()

    barrier = pltpu.get_barrier_semaphore()
    peers = [core_dev, zl_dev, *x_dev.values(), *z_dev.values(), *y_dev.values()]
    for dev in peers:
        pl.semaphore_signal(barrier, inc=1, device_id=dev, device_id_type=MESH)
    hbuf[zh, x, core] = jnp.transpose(h_ref[...].astype(F32)).astype(BF)
    pl.semaphore_wait(barrier, len(peers))

    def block(buf, q, i, c):
        return buf.at[(zh + q) % NZ, (x + i) % NX, c]

    def spread(buf, name, q):
        mine = block(buf, q, 0, core)
        for i in far:
            send(mine, mine, (name, "x", (NX - i) % NX, q), x_dev[i])
        send(mine, mine, (name, "c", 0, q), core_dev)

    def gather_start(buf, name):
        mine = block(buf, 0, 0, core)
        for q in far:
            send(mine, mine, (name, "z", (NZ - q) % NZ), z_dev[q])
        spread(buf, name, 0)

    def from_z(buf, name, q):
        arrive(block(buf, q, 0, core), (name, "z", q))
        spread(buf, name, q)

    def from_x(buf, name, q):
        for i in far:
            got = block(buf, q, i, core)
            arrive(got, (name, "x", i, q))
            send(got, got, (name, "c", i, q), core_dev)

    def from_core(buf, name, q):
        for i in range(NX):
            arrive(block(buf, q, i, mate), (name, "c", i, q))

    gather_start(hbuf, "h")
    loads[0].wait()
    loads[1].wait()
    for i in range(32):
        wt[:, i * B:(i + 1) * B] = jnp.transpose(w[i * B:(i + 1) * B, :].astype(F32)).astype(BF)
    for i in range(4):
        et[i * B:(i + 1) * B, :] = jnp.transpose(e[:, i * B:(i + 1) * B].astype(F32)).astype(BF)
    for copy in loads[2:]:
        copy.wait()

    def to_planes(q):
        zq = (zh + q) % NZ
        near_by = (zq + NY - y) % NZ
        for k, ahead in enumerate((near_by + NZ, near_by)):
            copy = pltpu.make_async_remote_copy(
                hbuf.at[zq, :, core],
                fy.at[y, :, core],
                fsend.at[q, k],
                frecv.at[(NY - ahead) % NY],
                device_id=(zl * NY + (y + ahead) % NY, t),
                device_id_type=MESH,
            )
            if k:
                pl.when(near_by != 0)(copy.start)
                planes.append((near_by != 0, copy))
            else:
                copy.start()
                planes.append((None, copy))

    planes = []
    from_z(hbuf, "h", 1)
    from_z(hbuf, "h", 3)
    from_x(hbuf, "h", 0)
    to_planes(0)
    from_z(hbuf, "h", 2)
    from_x(hbuf, "h", 1)
    to_planes(1)
    from_x(hbuf, "h", 3)
    to_planes(3)
    from_x(hbuf, "h", 2)
    to_planes(2)
    for q in (0, 1, 3, 2):
        from_core(hbuf, "h", q)

    pbuf[zh, x, core] = dot(wt[...], hbuf[...].reshape(32 * B, B)).astype(BF)
    gather_start(pbuf, "p")
    def core_step(p, r, name, q):
        send(p.at[q, mate], r.at[q], (name, "c", q), core_dev)

    def x_step(p, r, s, xr, name, q):
        arrive(r.at[q], (name, "c", q))
        for i in (*far, 0):
            there = (x + i) % NX
            total = p[q, core, there].astype(F32) + r[q, there].astype(F32)
            s[q, i] = total.astype(BF)
            if i:
                send(s.at[q, i], xr.at[q, NX - i], (name, "x", NX - i, q), x_dev[i])

    def z_step(s, xr, s2, zr, name, q):
        total = s[q, 0].astype(F32)
        for i in far:
            arrive(xr.at[q, i], (name, "x", i, q))
            total += xr[q, i].astype(F32)
        if q:
            s2[q] = total.astype(BF)
            send(s2.at[q], zr.at[NZ - q], (name, "z", NZ - q), z_dev[q])
        return total

    def last_step(total, zr, name):
        for q in far:
            arrive(zr.at[q], (name, "z", q))
            total += zr[q].astype(F32)
        return total

    offset = off[...].astype(F32) * (1.0 / SPAN)
    event = (1 - cen[...]).astype(F32)
    piece = ep[...]

    def grads(q):
        zq = (zh + q) % NZ
        for h in range(2):
            p = zq * 2 + h
            proj = pbuf[zq, 2 * h:2 * h + 2].reshape(4 * B, B)
            logits = dot(e[...], proj)
            inside = piece == p
            exposure = jnp.where(piece > p, 1.0, jnp.where(inside, offset, 0.0))
            grad = (jnp.exp(logits) * exposure - jnp.where(inside, event, 0.0)) * scale
            grad = grad.astype(BF)
            lg[p] = grad
            out = dot(et[...], grad).astype(BF)
            for j in range(4):
                part[q, j % 2, 2 * h + j // 2] = out[j * B:(j + 1) * B]
        core_step(part, crecv, "g", q)

    def reduce_x(q):
        x_step(part, crecv, s1, xrecv, "g", q)

    from_z(pbuf, "p", 1)
    from_z(pbuf, "p", 3)
    from_x(pbuf, "p", 0)
    from_z(pbuf, "p", 2)
    from_core(pbuf, "p", 0)
    grads(0)
    from_x(pbuf, "p", 1)
    from_x(pbuf, "p", 3)
    reduce_x(0)
    from_core(pbuf, "p", 1)
    grads(1)
    from_x(pbuf, "p", 2)
    from_core(pbuf, "p", 3)
    grads(3)
    reduce_x(1)
    from_core(pbuf, "p", 2)
    grads(2)
    reduce_x(3)
    reduce_x(2)

    total = jnp.zeros(e.shape, F32)
    for p in range(8):
        total += dot_nt(lg[p], pbuf[p // 2, 2 * (p % 2):2 * (p % 2) + 2].reshape(4 * B, B))
    epart[...] = total.astype(BF).reshape(epart.shape)
    for i in far_y:
        send(epart.at[(y + i) % NY], erecv.at[NY - i], ("e", NY - i), y_dev[i])

    for q in (1, 3, 2):
        z_step(s1, xrecv, s2, zrecv, "g", q)
    total = z_step(s1, xrecv, s2, zrecv, "g", 0)
    total = last_step(total, zrecv, "g")
    grad = total.astype(BF)
    pg[...] = jnp.transpose(total).astype(BF)
    for i in far_y:
        send(pg, pgy.at[y], ("pg", NY - i), y_dev[i])

    def hidden(q):
        zq = (zh + q) % NZ
        first = pl.multiple_of(zq * 2 * NX * B, 2 * NX * B)
        out = dot(w[pl.ds(first, 2 * NX * B), :], grad).astype(BF)
        for j in range(2 * NX):
            hpart[q, j % 2, j // 2] = out[j * B:(j + 1) * B]
        core_step(hpart, hcrecv, "d", q)

    hidden(2)
    hidden(1)
    x_step(hpart, hcrecv, hs1, hxrecv, "d", 2)
    hidden(3)
    x_step(hpart, hcrecv, hs1, hxrecv, "d", 1)
    hidden(0)
    x_step(hpart, hcrecv, hs1, hxrecv, "d", 3)
    x_step(hpart, hcrecv, hs1, hxrecv, "d", 0)

    total = epart[y].astype(F32)
    for i in far_y:
        arrive(erecv.at[i], ("e", i))
        total += erecv[i].astype(F32)
    eown[...] = total.astype(BF)
    send(eown, epeer, ("ez",), zl_dev)

    chunk = y % NZ
    for i in far_y:
        got = fy.at[(y + i) % NY, :, core]
        pltpu.make_async_remote_copy(
            got, got, fsend.at[0, 0], frecv.at[i], device_id=core_dev, device_id_type=MESH
        ).wait_recv()
        send(got, got, ("fc", i), core_dev)
    fy[y] = hbuf[chunk]
    pgy[y] = pg[...]

    arrive(epeer, ("ez",))
    eg_ref[y] = (eown[...].astype(F32) + epeer[...].astype(F32)).astype(BF)
    for i in far_y:
        send(eg_ref.at[y], eg_ref.at[y], ("ey", NY - i), y_dev[i])

    def half(ref, j, c):
        return ref.at[j, c] if j < 2 else ref.at[j]

    for i in far_y:
        arrive(fy.at[(y + i) % NY, :, mate], ("fc", i))
    for i in far_y:
        arrive(pgy.at[(y + i) % NY], ("pg", i))
    for j in range(NX):
        total = jnp.zeros((2 * B, B), F32)
        for i in range(0, NY, 2):
            feats = jnp.concatenate([fy[k, j].reshape(2 * B, B) for k in (i, i + 1)], 1)
            total += dot(feats, jnp.concatenate([pgy[i], pgy[i + 1]], 0))
        wown[j] = total.astype(BF).reshape(2, B, B)
        send(half(wown, j, 1 - zl), half(wpeer, j, 1 - zl), ("wz", j), zl_dev)

    for q in (1, 3, 2):
        z_step(hs1, hxrecv, hs2, hzrecv, "d", q)
    hidden_total = z_step(hs1, hxrecv, hs2, hzrecv, "d", 0)

    def pass_on(i, j):
        got = half(wg_ref.at[(chunk + i) % NZ], j, zl)
        send(got, got, ("wf", i, j), zl_dev)

    for j in range(NX):
        arrive(half(wpeer, j, zl), ("wz", j))
        mine = half(wg_ref.at[chunk], j, zl)
        mine[...] = (half(wown, j, zl)[...].astype(F32) + half(wpeer, j, zl)[...].astype(F32)).astype(BF)
        for i in (6 if j % 2 else 2, 1, 7):
            send(mine, mine, ("wy", NY - i, j), y_dev[i])
        if j < 2:
            pass_on(0, j)
        store(mine, half(wg_hbm.at[chunk], j, zl))

    hg_ref[...] = last_step(hidden_total, hzrecv, "d").astype(BF)
    store(hg_ref, hg_hbm)

    for i in far_y:
        arrive(eg_ref.at[(y + i) % NY], ("ey", i))
    store(eg_ref, eg_hbm)
    for j in range(NX):
        for i in (1, 7, 2 if j % 2 else 6):
            there = (chunk + i) % NZ
            arrive(half(wg_ref.at[there], j, zl), ("wy", i, j))
            if j < 2:
                pass_on(i, j)
            store(half(wg_ref.at[there], j, zl), half(wg_hbm.at[there], j, zl))
    for j in range(2):
        for i in (0, 1, 7, 2 if j % 2 else 6):
            there = (chunk + i) % NZ
            arrive(wg_ref.at[there, j, 1 - zl], ("wf", i, j))
            store(wg_ref.at[there, j, 1 - zl], wg_hbm.at[there, j, 1 - zl])
    for copy in stored:
        copy.wait()
    for copy in sent:
        copy.wait_send()
    for there, copy in planes:
        if there is None:
            copy.wait_send()
        else:
            pl.when(there)(copy.wait_send)
    assert len(sent) <= NSEM and len(ids) <= NSEM


def move_kernel(hg, wg, eg, hg_out, wg_out, eg_out, hg_v, wg_v, eg_v, isem, osem):
    moves = [(wg.at[i], wg_v.at[i], wg_out.at[i]) for i in range(NZ)]
    moves += [(eg, eg_v, eg_out), (hg, hg_v, hg_out)]
    loads = [pltpu.make_async_copy(a, b, isem.at[i]) for i, (a, b, _) in enumerate(moves)]
    stores = [pltpu.make_async_copy(b, c, osem.at[i]) for i, (_, b, c) in enumerate(moves)]
    for copy in loads:
        copy.start()
    for load, save in zip(loads, stores):
        load.wait()
        save.start()
    for copy in stores:
        copy.wait()


def move_results(*results):
    anywhere = [pl.BlockSpec(memory_space=pl.ANY)] * 3
    return pl.pallas_call(
        move_kernel,
        out_shape=[jax.ShapeDtypeStruct(r.shape, r.dtype) for r in results],
        in_specs=anywhere,
        out_specs=anywhere,
        scratch_shapes=[
            *[pltpu.VMEM(r.shape, r.dtype) for r in results],
            pltpu.SemaphoreType.DMA((NZ + 2,)),
            pltpu.SemaphoreType.DMA((NZ + 2,)),
        ],
        compiler_params=pltpu.CompilerParams(vmem_limit_bytes=62 * 2**20),
    )(*results)


def shards(hidden, proj_weight, task_embed, event_piece, censored, offset):
    rows = hidden.shape[0]
    scale = 1.0 / math.sqrt(rows * lax.axis_size("dp"))
    tasks, rank = task_embed.shape
    features, cols = proj_weight.shape
    vmem = pl.BlockSpec(memory_space=pltpu.VMEM)
    hbm = pl.BlockSpec(memory_space=pl.ANY)

    def reduce_buffers():
        return [
            pltpu.VMEM((NZ, 2, NX, B, B), BF),
            pltpu.VMEM((NZ, NX, B, B), BF),
            pltpu.VMEM((NZ, NX, B, B), BF),
            pltpu.VMEM((NZ, NX, B, B), BF),
            pltpu.VMEM((NZ, B, B), BF),
            pltpu.VMEM((NZ, B, B), BF),
        ]

    hidden_grad, weight_grad, embed_grad = pl.pallas_call(
        functools.partial(kernel, scale),
        out_shape=(
            jax.ShapeDtypeStruct((B, rows), BF),
            jax.ShapeDtypeStruct((NZ, NX, 2, B, cols), BF),
            jax.ShapeDtypeStruct((NY, tasks // NY, rank), BF),
        ),
        in_specs=[vmem] + [hbm] * 5,
        out_specs=(hbm, hbm, hbm),
        scratch_shapes=[
            pltpu.VMEM((features, cols), BF),
            pltpu.VMEM((tasks, rank), BF),
            pltpu.VMEM((tasks, rows), jnp.int32),
            pltpu.VMEM((tasks, rows), jnp.int32),
            pltpu.VMEM((tasks, rows), jnp.int32),
            pltpu.VMEM((cols, features), BF),
            pltpu.VMEM((rank, tasks), BF),
            pltpu.VMEM((NZ, NX, 2, B, B), BF),
            pltpu.VMEM((NZ, NX, 2, B, B), BF),
            pltpu.VMEM((8, tasks, rows), BF),
            pltpu.VMEM((NY, NX, 2, B, B), BF),
            *reduce_buffers(),
            *reduce_buffers(),
            pltpu.VMEM((B, B), BF),
            pltpu.VMEM((NY, B, B), BF),
            pltpu.VMEM((NX, 2, B, B), BF),
            pltpu.VMEM((NX, 2, B, B), BF),
            pltpu.VMEM((NY, tasks // NY, rank), BF),
            pltpu.VMEM((NY, tasks // NY, rank), BF),
            pltpu.VMEM((tasks // NY, rank), BF),
            pltpu.VMEM((tasks // NY, rank), BF),
            pltpu.VMEM((B, rows), BF),
            pltpu.VMEM((NZ, NX, 2, B, cols), BF),
            pltpu.VMEM((NY, tasks // NY, rank), BF),
            pltpu.SemaphoreType.DMA((5,)),
            pltpu.SemaphoreType.DMA((32,)),
            pltpu.SemaphoreType.DMA((NZ, 2)),
            pltpu.SemaphoreType.DMA((NY,)),
            pltpu.SemaphoreType.DMA((NSEM,)),
            pltpu.SemaphoreType.DMA((NSEM,)),
        ],
        compiler_params=pltpu.CompilerParams(
            collective_id=0, has_side_effects=True, vmem_limit_bytes=62 * 2**20
        ),
    )(hidden, proj_weight, task_embed, event_piece, censored, offset)
    hidden_grad, weight_grad, embed_grad = move_results(hidden_grad, weight_grad, embed_grad)
    return (
        hidden_grad,
        weight_grad.reshape(features, cols),
        embed_grad.reshape(tasks, rank),
    )


def solution(mesh):
    return jax.shard_map(
        shards,
        mesh=mesh,
        in_specs=(
            P("dp", "task"),
            P(None, "task"),
            P("task", None),
            P("task", "dp"),
            P("task", "dp"),
            P("task", "dp"),
        ),
        out_specs=(P("task", "dp"), P(None, "task"), P("task", None)),
        check_vma=False,
    )
```

```python
import functools
import math

import jax
import jax.numpy as jnp
from jax import lax
from jax.experimental import pallas as pl
from jax.experimental.pallas import tpu as pltpu
from jax.sharding import PartitionSpec as P

SPAN = 64
B = 128
NX = 4
NZ = 4
NY = 8
MESH = pl.DeviceIdType.MESH
BF = jnp.bfloat16
F32 = jnp.float32
NSEM = 224


def dot(a, b):
    return jnp.dot(a, b, preferred_element_type=F32)


def dot_nt(a, b):
    return lax.dot_general(a, b, (((1,), (1,)), ((), ())), preferred_element_type=F32)


def kernel(
    scale,
    h_hbm, w_hbm, e_hbm, ep_hbm, cen_hbm, off_hbm,
    hg_hbm, wg_hbm, eg_hbm,
    w, e, ep, cen, off, et, hbuf, pbuf, lg, fy, ht,
    part, crecv, s1, xrecv, s2, zrecv,
    hpart, hcrecv, hs1, hxrecv, hs2, hzrecv,
    pg, pgy, wown, wpeer, epart, erecv, eown, epeer,
    hg_ref, wg_ref, eg_ref,
    lsem, osem, fsend, frecv, ssem, rsem,
):
    dp = lax.axis_index("dp")
    t = lax.axis_index("task")
    y, zl = dp % NY, dp // NY
    core, x, zh = t % 2, (t // 2) % NX, t // (2 * NX)
    mate = 1 - core

    core_dev = (dp, t + 1 - 2 * core)
    x_dev = {i: (dp, zh * 2 * NX + ((x + i) % NX) * 2 + core) for i in range(1, NX)}
    z_dev = {i: (dp, ((zh + i) % NZ) * 2 * NX + x * 2 + core) for i in range(1, NZ)}
    y_dev = {i: (zl * NY + (y + i) % NY, t) for i in range(1, NY)}
    zl_dev = ((1 - zl) * NY + y, t)
    far_y = (4, 3, 5, 2, 6, 1, 7)
    far = (1, 3, 2)

    ids = {}
    sent = []
    stored = []

    def store(src, dst):
        copy = pltpu.make_async_copy(src, dst, osem.at[len(stored)])
        copy.start()
        stored.append(copy)

    def send(src, dst, key, dev):
        slot = ids.setdefault(key, len(ids))
        copy = pltpu.make_async_remote_copy(
            src, dst, ssem.at[len(sent)], rsem.at[slot], device_id=dev, device_id_type=MESH
        )
        copy.start()
        sent.append(copy)

    def arrive(dst, key):
        slot = ids.setdefault(key, len(ids))
        pltpu.make_async_remote_copy(
            dst, dst, ssem.at[0], rsem.at[slot], device_id=core_dev, device_id_type=MESH
        ).wait_recv()

    barrier = pltpu.get_barrier_semaphore()
    peers = [core_dev, zl_dev, *x_dev.values(), *z_dev.values(), *y_dev.values()]
    for dev in peers:
        pl.semaphore_signal(barrier, inc=1, device_id=dev, device_id_type=MESH)
    loads = [
        pltpu.make_async_copy(src, dst, lsem.at[i])
        for i, (src, dst) in enumerate(
            ((h_hbm, hbuf.at[zh, x, core]), (w_hbm, w), (e_hbm, e), (ep_hbm, ep), (cen_hbm, cen), (off_hbm, off))
        )
    ]
    for copy in loads:
        copy.start()
    pl.semaphore_wait(barrier, len(peers))

    def block(buf, q, i, c):
        return buf.at[(zh + q) % NZ, (x + i) % NX, c]

    def spread(buf, name, q, src=None):
        mine = block(buf, q, 0, core)
        src = mine if src is None else src
        for i in far:
            send(src, mine, (name, "x", (NX - i) % NX, q), x_dev[i])
        send(src, mine, (name, "c", 0, q), core_dev)

    def gather_start(buf, name, src=None):
        mine = block(buf, 0, 0, core)
        src = mine if src is None else src
        for q in far:
            send(src, mine, (name, "z", (NZ - q) % NZ), z_dev[q])
        spread(buf, name, 0, src)

    def from_z(buf, name, q):
        arrive(block(buf, q, 0, core), (name, "z", q))
        spread(buf, name, q)

    def from_x(buf, name, q):
        for i in far:
            got = block(buf, q, i, core)
            arrive(got, (name, "x", i, q))
            send(got, got, (name, "c", i, q), core_dev)

    def from_core(buf, name, q):
        for i in range(NX):
            arrive(block(buf, q, i, mate), (name, "c", i, q))

    gather_start(hbuf, "h", h_hbm)
    for copy in loads:
        copy.wait()
    for i in range(4):
        et[i * B:(i + 1) * B, :] = jnp.transpose(e[:, i * B:(i + 1) * B].astype(F32)).astype(BF)
    def to_planes(q):
        zq = (zh + q) % NZ
        near_by = (zq + NY - y) % NZ
        for i in range(NX):
            ht[zq, i] = jnp.transpose(hbuf[zq, i, core].astype(F32)).astype(BF)
        for k, ahead in enumerate((near_by + NZ, near_by)):
            copy = pltpu.make_async_remote_copy(
                ht.at[zq],
                fy.at[y, :, core],
                fsend.at[q, k],
                frecv.at[(NY - ahead) % NY],
                device_id=(zl * NY + (y + ahead) % NY, t),
                device_id_type=MESH,
            )
            if k:
                pl.when(near_by != 0)(copy.start)
                planes.append((near_by != 0, copy))
            else:
                copy.start()
                planes.append((None, copy))

    planes = []
    from_z(hbuf, "h", 1)
    from_z(hbuf, "h", 3)
    from_x(hbuf, "h", 0)
    to_planes(0)
    from_z(hbuf, "h", 2)
    from_x(hbuf, "h", 1)
    to_planes(1)
    from_x(hbuf, "h", 3)
    to_planes(3)
    from_x(hbuf, "h", 2)
    to_planes(2)
    for q in (0, 1, 3, 2):
        from_core(hbuf, "h", q)

    feats = [hbuf[i // 8, (i // 2) % NX, i % 2] for i in range(8 * NZ)]
    pbuf[zh, x, core] = jnp.transpose(dot(jnp.concatenate(feats, 1), w[...])).astype(BF)
    gather_start(pbuf, "p")
    def core_step(p, r, name, q):
        send(p.at[q, mate], r.at[q], (name, "c", q), core_dev)

    def x_step(p, r, s, xr, name, q):
        arrive(r.at[q], (name, "c", q))
        for i in (*far, 0):
            there = (x + i) % NX
            total = p[q, core, there].astype(F32) + r[q, there].astype(F32)
            s[q, i] = total.astype(BF)
            if i:
                send(s.at[q, i], xr.at[q, NX - i], (name, "x", NX - i, q), x_dev[i])

    def z_step(s, xr, s2, zr, name, q):
        total = s[q, 0].astype(F32)
        for i in far:
            arrive(xr.at[q, i], (name, "x", i, q))
            total += xr[q, i].astype(F32)
        if q:
            s2[q] = total.astype(BF)
            send(s2.at[q], zr.at[NZ - q], (name, "z", NZ - q), z_dev[q])
        return total

    def last_step(total, zr, name):
        for q in far:
            arrive(zr.at[q], (name, "z", q))
            total += zr[q].astype(F32)
        return total

    offset = off[...].astype(F32) * (1.0 / SPAN)
    event = (1 - cen[...]).astype(F32)
    piece = ep[...]

    def grads(q):
        zq = (zh + q) % NZ
        def one_piece(h, carry):
            p = zq * 2 + h
            proj = pbuf[zq, pl.ds(2 * h, 2)].reshape(4 * B, B)
            logits = dot(e[...], proj)
            inside = piece == p
            exposure = jnp.where(piece > p, 1.0, jnp.where(inside, offset, 0.0))
            grad = (jnp.exp(logits) * exposure - jnp.where(inside, event, 0.0)) * scale
            grad = grad.astype(BF)
            lg[p] = grad
            out = dot(et[...], grad).astype(BF)
            for j in range(4):
                part[q, j % 2, 2 * h + j // 2] = out[j * B:(j + 1) * B]
            return carry

        lax.fori_loop(0, 2, one_piece, 0)
        core_step(part, crecv, "g", q)

    def reduce_x(q):
        x_step(part, crecv, s1, xrecv, "g", q)

    from_z(pbuf, "p", 1)
    from_z(pbuf, "p", 3)
    from_x(pbuf, "p", 0)
    from_z(pbuf, "p", 2)
    from_core(pbuf, "p", 0)
    grads(0)
    from_x(pbuf, "p", 1)
    from_x(pbuf, "p", 3)
    reduce_x(0)
    from_core(pbuf, "p", 1)
    grads(1)
    from_x(pbuf, "p", 2)
    from_core(pbuf, "p", 3)
    grads(3)
    reduce_x(1)
    from_core(pbuf, "p", 2)
    grads(2)
    reduce_x(3)
    reduce_x(2)

    total = jnp.zeros(e.shape, F32)
    for p in range(8):
        total += dot_nt(lg[p], pbuf[p // 2, 2 * (p % 2):2 * (p % 2) + 2].reshape(4 * B, B))
    epart[...] = total.astype(BF).reshape(epart.shape)
    for i in far_y:
        send(epart.at[(y + i) % NY], erecv.at[NY - i], ("e", NY - i), y_dev[i])

    for q in (1, 3, 2):
        z_step(s1, xrecv, s2, zrecv, "g", q)
    total = z_step(s1, xrecv, s2, zrecv, "g", 0)
    total = last_step(total, zrecv, "g")
    grad = total.astype(BF)
    pg[...] = jnp.transpose(total).astype(BF)
    for i in far_y:
        send(pg, pgy.at[y], ("pg", NY - i), y_dev[i])

    def hidden(q):
        zq = (zh + q) % NZ
        first = pl.multiple_of(zq * 2 * NX * B, 2 * NX * B)
        out = dot(w[pl.ds(first, 2 * NX * B), :], grad).astype(BF)
        for j in range(2 * NX):
            hpart[q, j % 2, j // 2] = out[j * B:(j + 1) * B]
        core_step(hpart, hcrecv, "d", q)

    hidden(2)
    hidden(1)
    x_step(hpart, hcrecv, hs1, hxrecv, "d", 2)
    hidden(3)
    x_step(hpart, hcrecv, hs1, hxrecv, "d", 1)
    hidden(0)
    x_step(hpart, hcrecv, hs1, hxrecv, "d", 3)
    x_step(hpart, hcrecv, hs1, hxrecv, "d", 0)

    total = epart[y].astype(F32)
    for i in far_y:
        arrive(erecv.at[i], ("e", i))
        total += erecv[i].astype(F32)
    eown[...] = total.astype(BF)
    send(eown, epeer, ("ez",), zl_dev)

    chunk = y % NZ
    for i in far_y:
        got = fy.at[(y + i) % NY, :, core]
        pltpu.make_async_remote_copy(
            got, got, fsend.at[0, 0], frecv.at[i], device_id=core_dev, device_id_type=MESH
        ).wait_recv()
        send(got, got, ("fc", i), core_dev)
    for i in range(NX):
        fy[y, i, core] = ht[chunk, i]
        fy[y, i, mate] = jnp.transpose(hbuf[chunk, i, mate].astype(F32)).astype(BF)
    pgy[y] = pg[...]

    arrive(epeer, ("ez",))
    eg_ref[y] = (eown[...].astype(F32) + epeer[...].astype(F32)).astype(BF)
    for i in far_y:
        send(eg_ref.at[y], eg_ref.at[y], ("ey", NY - i), y_dev[i])

    def half(ref, j, c):
        return ref.at[j, c] if j < 2 else ref.at[j]

    for i in far_y:
        arrive(fy.at[(y + i) % NY, :, mate], ("fc", i))
    for i in far_y:
        arrive(pgy.at[(y + i) % NY], ("pg", i))
    for j in range(NX):
        total = jnp.zeros((2 * B, B), F32)
        for i in range(0, NY, 2):
            feats = jnp.concatenate([fy[k, j].reshape(2 * B, B) for k in (i, i + 1)], 1)
            total += dot(feats, jnp.concatenate([pgy[i], pgy[i + 1]], 0))
        wown[j] = total.astype(BF).reshape(2, B, B)
        send(half(wown, j, 1 - zl), half(wpeer, j, 1 - zl), ("wz", j), zl_dev)

    for q in (1, 3, 2):
        z_step(hs1, hxrecv, hs2, hzrecv, "d", q)
    hidden_total = z_step(hs1, hxrecv, hs2, hzrecv, "d", 0)

    def pass_on(i, j):
        got = half(wg_ref.at[(chunk + i) % NZ], j, zl)
        send(got, got, ("wf", i, j), zl_dev)

    for j in range(NX):
        arrive(half(wpeer, j, zl), ("wz", j))
        mine = half(wg_ref.at[chunk], j, zl)
        mine[...] = (half(wown, j, zl)[...].astype(F32) + half(wpeer, j, zl)[...].astype(F32)).astype(BF)
        for i in (6 if j % 2 else 2, 1, 7):
            send(mine, mine, ("wy", NY - i, j), y_dev[i])
        if j < 2:
            pass_on(0, j)
        store(mine, half(wg_hbm.at[chunk], j, zl))

    hg_ref[...] = last_step(hidden_total, hzrecv, "d").astype(BF)
    store(hg_ref, hg_hbm)

    for i in far_y:
        arrive(eg_ref.at[(y + i) % NY], ("ey", i))
    store(eg_ref, eg_hbm)
    for j in range(NX):
        for i in (1, 7, 2 if j % 2 else 6):
            there = (chunk + i) % NZ
            arrive(half(wg_ref.at[there], j, zl), ("wy", i, j))
            if j < 2:
                pass_on(i, j)
            store(half(wg_ref.at[there], j, zl), half(wg_hbm.at[there], j, zl))
    for j in range(2):
        for i in (0, 1, 7, 2 if j % 2 else 6):
            there = (chunk + i) % NZ
            arrive(wg_ref.at[there, j, 1 - zl], ("wf", i, j))
            store(wg_ref.at[there, j, 1 - zl], wg_hbm.at[there, j, 1 - zl])
    for copy in stored:
        copy.wait()
    for copy in sent:
        copy.wait_send()
    for there, copy in planes:
        if there is None:
            copy.wait_send()
        else:
            pl.when(there)(copy.wait_send)
    assert len(sent) <= NSEM and len(ids) <= NSEM


def move_kernel(hg, wg, eg, hg_out, wg_out, eg_out, hg_v, wg_v, eg_v, isem, osem):
    moves = [(wg.at[i], wg_v.at[i], wg_out.at[i]) for i in range(NZ)]
    moves += [(eg, eg_v, eg_out), (hg, hg_v, hg_out)]
    loads = [pltpu.make_async_copy(a, b, isem.at[i]) for i, (a, b, _) in enumerate(moves)]
    stores = [pltpu.make_async_copy(b, c, osem.at[i]) for i, (_, b, c) in enumerate(moves)]
    for copy in loads:
        copy.start()
    for load, save in zip(loads, stores):
        load.wait()
        save.start()
    for copy in stores:
        copy.wait()


def move_results(*results):
    anywhere = [pl.BlockSpec(memory_space=pl.ANY)] * 3
    return pl.pallas_call(
        move_kernel,
        out_shape=[jax.ShapeDtypeStruct(r.shape, r.dtype) for r in results],
        in_specs=anywhere,
        out_specs=anywhere,
        scratch_shapes=[
            *[pltpu.VMEM(r.shape, r.dtype) for r in results],
            pltpu.SemaphoreType.DMA((NZ + 2,)),
            pltpu.SemaphoreType.DMA((NZ + 2,)),
        ],
        compiler_params=pltpu.CompilerParams(vmem_limit_bytes=62 * 2**20),
    )(*results)


def shards(hidden, proj_weight, task_embed, event_piece, censored, offset):
    rows = hidden.shape[0]
    scale = 1.0 / math.sqrt(rows * lax.axis_size("dp"))
    tasks, rank = task_embed.shape
    features, cols = proj_weight.shape
    hbm = pl.BlockSpec(memory_space=pl.ANY)

    def reduce_buffers():
        return [
            pltpu.VMEM((NZ, 2, NX, B, B), BF),
            pltpu.VMEM((NZ, NX, B, B), BF),
            pltpu.VMEM((NZ, NX, B, B), BF),
            pltpu.VMEM((NZ, NX, B, B), BF),
            pltpu.VMEM((NZ, B, B), BF),
            pltpu.VMEM((NZ, B, B), BF),
        ]

    hidden_grad, weight_grad, embed_grad = pl.pallas_call(
        functools.partial(kernel, scale),
        out_shape=(
            jax.ShapeDtypeStruct((B, rows), BF),
            jax.ShapeDtypeStruct((NZ, NX, 2, B, cols), BF),
            jax.ShapeDtypeStruct((NY, tasks // NY, rank), BF),
        ),
        in_specs=[hbm] * 6,
        out_specs=(hbm, hbm, hbm),
        scratch_shapes=[
            pltpu.VMEM((features, cols), BF),
            pltpu.VMEM((tasks, rank), BF),
            pltpu.VMEM((tasks, rows), jnp.int32),
            pltpu.VMEM((tasks, rows), jnp.int32),
            pltpu.VMEM((tasks, rows), jnp.int32),
            pltpu.VMEM((rank, tasks), BF),
            pltpu.VMEM((NZ, NX, 2, B, B), BF),
            pltpu.VMEM((NZ, NX, 2, B, B), BF),
            pltpu.VMEM((8, tasks, rows), BF),
            pltpu.VMEM((NY, NX, 2, B, B), BF),
            pltpu.VMEM((NZ, NX, B, B), BF),
            *reduce_buffers(),
            *reduce_buffers(),
            pltpu.VMEM((B, B), BF),
            pltpu.VMEM((NY, B, B), BF),
            pltpu.VMEM((NX, 2, B, B), BF),
            pltpu.VMEM((NX, 2, B, B), BF),
            pltpu.VMEM((NY, tasks // NY, rank), BF),
            pltpu.VMEM((NY, tasks // NY, rank), BF),
            pltpu.VMEM((tasks // NY, rank), BF),
            pltpu.VMEM((tasks // NY, rank), BF),
            pltpu.VMEM((B, rows), BF),
            pltpu.VMEM((NZ, NX, 2, B, cols), BF),
            pltpu.VMEM((NY, tasks // NY, rank), BF),
            pltpu.SemaphoreType.DMA((6,)),
            pltpu.SemaphoreType.DMA((32,)),
            pltpu.SemaphoreType.DMA((NZ, 2)),
            pltpu.SemaphoreType.DMA((NY,)),
            pltpu.SemaphoreType.DMA((NSEM,)),
            pltpu.SemaphoreType.DMA((NSEM,)),
        ],
        compiler_params=pltpu.CompilerParams(
            collective_id=0, has_side_effects=True, vmem_limit_bytes=62 * 2**20
        ),
    )(hidden, proj_weight, task_embed, event_piece, censored, offset)
    hidden_grad, weight_grad, embed_grad = move_results(hidden_grad, weight_grad, embed_grad)
    return (
        hidden_grad,
        weight_grad.reshape(features, cols),
        embed_grad.reshape(tasks, rank),
    )


def solution(mesh):
    return jax.shard_map(
        shards,
        mesh=mesh,
        in_specs=(
            P("dp", "task"),
            P(None, "task"),
            P("task", None),
            P("task", "dp"),
            P("task", "dp"),
            P("task", "dp"),
        ),
        out_specs=(P("task", "dp"), P(None, "task"), P("task", None)),
        check_vma=False,
    )
```

```python
import functools
import math

import jax
import jax.numpy as jnp
from jax import lax
from jax.experimental import pallas as pl
from jax.experimental.pallas import tpu as pltpu
from jax.sharding import PartitionSpec as P

SPAN = 64
B = 128
NX = 4
NZ = 4
NY = 8
MESH = pl.DeviceIdType.MESH
BF = jnp.bfloat16
F32 = jnp.float32
NSEM = 224


def dot(a, b):
    return jnp.dot(a, b, preferred_element_type=F32)


def dot_nt(a, b):
    return lax.dot_general(a, b, (((1,), (1,)), ((), ())), preferred_element_type=F32)


def kernel(
    scale,
    h_hbm, w_hbm, e_hbm, ep_hbm, cen_hbm, off_hbm,
    hg_hbm, wg_hbm, eg_hbm,
    w, e, ep, cen, off, et, hbuf, pbuf, lg, fy, ht,
    part, crecv, s1, xrecv, s2, zrecv,
    hpart, hcrecv, hs1, hxrecv, hs2, hzrecv,
    pg, pgy, wown, wpeer, epart, erecv, eown, epeer,
    hg_ref, wg_ref, eg_ref,
    lsem, osem, fsend, frecv, ssem, rsem,
):
    dp = lax.axis_index("dp")
    t = lax.axis_index("task")
    y, zl = dp % NY, dp // NY
    core, x, zh = t % 2, (t // 2) % NX, t // (2 * NX)
    mate = 1 - core

    core_dev = (dp, t + 1 - 2 * core)
    x_dev = {i: (dp, zh * 2 * NX + ((x + i) % NX) * 2 + core) for i in range(1, NX)}
    z_dev = {i: (dp, ((zh + i) % NZ) * 2 * NX + x * 2 + core) for i in range(1, NZ)}
    y_dev = {i: (zl * NY + (y + i) % NY, t) for i in range(1, NY)}
    zl_dev = ((1 - zl) * NY + y, t)
    far_y = (4, 3, 5, 2, 6, 1, 7)
    far = (1, 3, 2)

    ids = {}
    sent = []
    stored = []

    def store(src, dst):
        copy = pltpu.make_async_copy(src, dst, osem.at[len(stored)])
        copy.start()
        stored.append(copy)

    def send(src, dst, key, dev):
        slot = ids.setdefault(key, len(ids))
        copy = pltpu.make_async_remote_copy(
            src, dst, ssem.at[len(sent)], rsem.at[slot], device_id=dev, device_id_type=MESH
        )
        copy.start()
        sent.append(copy)

    def arrive(dst, key):
        slot = ids.setdefault(key, len(ids))
        pltpu.make_async_remote_copy(
            dst, dst, ssem.at[0], rsem.at[slot], device_id=core_dev, device_id_type=MESH
        ).wait_recv()

    barrier = pltpu.get_barrier_semaphore()
    peers = [core_dev, zl_dev, *x_dev.values(), *z_dev.values(), *y_dev.values()]
    for dev in peers:
        pl.semaphore_signal(barrier, inc=1, device_id=dev, device_id_type=MESH)
    loads = [
        pltpu.make_async_copy(src, dst, lsem.at[i])
        for i, (src, dst) in enumerate(
            ((h_hbm, hbuf.at[zh, x, core]), (w_hbm, w), (e_hbm, e), (ep_hbm, ep), (cen_hbm, cen), (off_hbm, off))
        )
    ]
    for copy in loads:
        copy.start()
    pl.semaphore_wait(barrier, len(peers))

    def block(buf, q, i, c):
        return buf.at[(zh + q) % NZ, (x + i) % NX, c]

    def spread(buf, name, q, src=None):
        mine = block(buf, q, 0, core)
        src = mine if src is None else src
        for i in far:
            send(src, mine, (name, "x", (NX - i) % NX, q), x_dev[i])
        send(src, mine, (name, "c", 0, q), core_dev)

    def gather_start(buf, name, src=None):
        mine = block(buf, 0, 0, core)
        src = mine if src is None else src
        for q in far:
            send(src, mine, (name, "z", (NZ - q) % NZ), z_dev[q])
        spread(buf, name, 0, src)

    def from_z(buf, name, q):
        arrive(block(buf, q, 0, core), (name, "z", q))
        spread(buf, name, q)

    def from_x(buf, name, q):
        for i in far:
            got = block(buf, q, i, core)
            arrive(got, (name, "x", i, q))
            send(got, got, (name, "c", i, q), core_dev)

    def from_core(buf, name, q):
        for i in range(NX):
            arrive(block(buf, q, i, mate), (name, "c", i, q))

    gather_start(hbuf, "h", h_hbm)
    for copy in loads:
        copy.wait()
    for i in range(4):
        et[i * B:(i + 1) * B, :] = jnp.transpose(e[:, i * B:(i + 1) * B].astype(F32)).astype(BF)
    def to_planes(q):
        zq = (zh + q) % NZ
        near_by = (zq + NY - y) % NZ
        for i in range(NX):
            ht[zq, i] = jnp.transpose(hbuf[zq, i, core].astype(F32)).astype(BF)
        for k, ahead in enumerate((near_by + NZ, near_by)):
            copy = pltpu.make_async_remote_copy(
                ht.at[zq],
                fy.at[y, :, core],
                fsend.at[q, k],
                frecv.at[(NY - ahead) % NY],
                device_id=(zl * NY + (y + ahead) % NY, t),
                device_id_type=MESH,
            )
            if k:
                pl.when(near_by != 0)(copy.start)
                planes.append((near_by != 0, copy))
            else:
                copy.start()
                planes.append((None, copy))

    planes = []
    from_z(hbuf, "h", 1)
    from_z(hbuf, "h", 3)
    from_x(hbuf, "h", 0)
    to_planes(0)
    from_z(hbuf, "h", 2)
    from_x(hbuf, "h", 1)
    to_planes(1)
    from_x(hbuf, "h", 3)
    to_planes(3)
    from_x(hbuf, "h", 2)
    to_planes(2)
    for q in (0, 1, 3, 2):
        from_core(hbuf, "h", q)

    feats = [hbuf[i // 8, (i // 2) % NX, i % 2] for i in range(8 * NZ)]
    pbuf[zh, x, core] = jnp.transpose(dot(jnp.concatenate(feats, 1), w[...])).astype(BF)
    gather_start(pbuf, "p")
    def core_step(p, r, name, q):
        send(p.at[q, mate], r.at[q], (name, "c", q), core_dev)

    def x_step(p, r, s, xr, name, q):
        arrive(r.at[q], (name, "c", q))
        for i in (*far, 0):
            there = (x + i) % NX
            total = p[q, core, there].astype(F32) + r[q, there].astype(F32)
            s[q, i] = total.astype(BF)
            if i:
                send(s.at[q, i], xr.at[q, NX - i], (name, "x", NX - i, q), x_dev[i])

    def z_step(s, xr, s2, zr, name, q):
        total = s[q, 0].astype(F32)
        for i in far:
            arrive(xr.at[q, i], (name, "x", i, q))
            total += xr[q, i].astype(F32)
        if q:
            s2[q] = total.astype(BF)
            send(s2.at[q], zr.at[NZ - q], (name, "z", NZ - q), z_dev[q])
        return total

    def last_step(total, zr, name):
        for q in far:
            arrive(zr.at[q], (name, "z", q))
            total += zr[q].astype(F32)
        return total

    offset = off[...].astype(F32) * (1.0 / SPAN)
    event = (1 - cen[...]).astype(F32)
    piece = ep[...]

    def grads(q):
        zq = (zh + q) % NZ
        def one_piece(h, carry):
            p = zq * 2 + h
            proj = pbuf[zq, pl.ds(2 * h, 2)].reshape(4 * B, B)
            logits = dot(e[...], proj)
            inside = piece == p
            exposure = jnp.where(piece > p, 1.0, jnp.where(inside, offset, 0.0))
            grad = (jnp.exp(logits) * exposure - jnp.where(inside, event, 0.0)) * scale
            grad = grad.astype(BF)
            lg[p] = grad
            out = dot(et[...], grad).astype(BF)
            for j in range(4):
                part[q, j % 2, 2 * h + j // 2] = out[j * B:(j + 1) * B]
            return carry

        lax.fori_loop(0, 2, one_piece, 0)
        core_step(part, crecv, "g", q)

    def reduce_x(q):
        x_step(part, crecv, s1, xrecv, "g", q)

    from_z(pbuf, "p", 1)
    from_z(pbuf, "p", 3)
    from_x(pbuf, "p", 0)
    from_z(pbuf, "p", 2)
    from_core(pbuf, "p", 0)
    grads(0)
    from_x(pbuf, "p", 1)
    from_x(pbuf, "p", 3)
    reduce_x(0)
    from_core(pbuf, "p", 1)
    grads(1)
    from_x(pbuf, "p", 2)
    from_core(pbuf, "p", 3)
    grads(3)
    reduce_x(1)
    from_core(pbuf, "p", 2)
    grads(2)
    reduce_x(3)
    reduce_x(2)

    total = jnp.zeros(e.shape, F32)
    for p in range(8):
        total += dot_nt(lg[p], pbuf[p // 2, 2 * (p % 2):2 * (p % 2) + 2].reshape(4 * B, B))
    epart[...] = total.astype(BF).reshape(epart.shape)
    for i in far_y:
        send(epart.at[(y + i) % NY], erecv.at[NY - i], ("e", NY - i), y_dev[i])

    for q in (1, 3, 2):
        z_step(s1, xrecv, s2, zrecv, "g", q)
    total = z_step(s1, xrecv, s2, zrecv, "g", 0)
    total = last_step(total, zrecv, "g")
    grad = total.astype(BF)
    pg[...] = jnp.transpose(total).astype(BF)
    for i in far_y:
        send(pg, pgy.at[y], ("pg", NY - i), y_dev[i])

    def hidden(q):
        zq = (zh + q) % NZ
        first = pl.multiple_of(zq * 2 * NX * B, 2 * NX * B)
        out = dot(w[pl.ds(first, 2 * NX * B), :], grad).astype(BF)
        for j in range(2 * NX):
            hpart[q, j % 2, j // 2] = out[j * B:(j + 1) * B]
        core_step(hpart, hcrecv, "d", q)

    hidden(2)
    hidden(1)
    x_step(hpart, hcrecv, hs1, hxrecv, "d", 2)
    hidden(3)
    x_step(hpart, hcrecv, hs1, hxrecv, "d", 1)
    hidden(0)
    x_step(hpart, hcrecv, hs1, hxrecv, "d", 3)
    x_step(hpart, hcrecv, hs1, hxrecv, "d", 0)

    chunk = y % NZ
    for i in far_y:
        got = fy.at[(y + i) % NY, :, core]
        pltpu.make_async_remote_copy(
            got, got, fsend.at[0, 0], frecv.at[i], device_id=core_dev, device_id_type=MESH
        ).wait_recv()
        send(got, got, ("fc", i), core_dev)

    total = epart[y].astype(F32)
    for i in far_y:
        arrive(erecv.at[i], ("e", i))
        total += erecv[i].astype(F32)
    eown[...] = total.astype(BF)
    send(eown, epeer, ("ez",), zl_dev)

    for i in range(NX):
        fy[y, i, core] = ht[chunk, i]
        fy[y, i, mate] = jnp.transpose(hbuf[chunk, i, mate].astype(F32)).astype(BF)
    pgy[y] = pg[...]

    arrive(epeer, ("ez",))
    eg_ref[y] = (eown[...].astype(F32) + epeer[...].astype(F32)).astype(BF)
    for i in far_y:
        send(eg_ref.at[y], eg_ref.at[y], ("ey", NY - i), y_dev[i])

    def half(ref, j, c):
        return ref.at[j, c] if j < 2 else ref.at[j]

    for i in far_y:
        arrive(fy.at[(y + i) % NY, :, mate], ("fc", i))
    for i in far_y:
        arrive(pgy.at[(y + i) % NY], ("pg", i))
    for j in range(NX):
        total = jnp.zeros((2 * B, B), F32)
        for i in range(0, NY, 2):
            feats = jnp.concatenate([fy[k, j].reshape(2 * B, B) for k in (i, i + 1)], 1)
            total += dot(feats, jnp.concatenate([pgy[i], pgy[i + 1]], 0))
        wown[j] = total.astype(BF).reshape(2, B, B)
        send(half(wown, j, 1 - zl), half(wpeer, j, 1 - zl), ("wz", j), zl_dev)

    for q in (1, 3, 2):
        z_step(hs1, hxrecv, hs2, hzrecv, "d", q)
    hidden_total = z_step(hs1, hxrecv, hs2, hzrecv, "d", 0)

    def pass_on(i, j):
        got = half(wg_ref.at[(chunk + i) % NZ], j, zl)
        send(got, got, ("wf", i, j), zl_dev)

    for j in range(NX):
        arrive(half(wpeer, j, zl), ("wz", j))
        mine = half(wg_ref.at[chunk], j, zl)
        mine[...] = (half(wown, j, zl)[...].astype(F32) + half(wpeer, j, zl)[...].astype(F32)).astype(BF)
        for i in (6 if j % 2 else 2, 1, 7):
            send(mine, mine, ("wy", NY - i, j), y_dev[i])
        if j < 2:
            pass_on(0, j)
        store(mine, half(wg_hbm.at[chunk], j, zl))

    hg_ref[...] = last_step(hidden_total, hzrecv, "d").astype(BF)
    store(hg_ref, hg_hbm)

    for i in far_y:
        arrive(eg_ref.at[(y + i) % NY], ("ey", i))
    store(eg_ref, eg_hbm)
    for j in range(NX):
        for i in (1, 7, 2 if j % 2 else 6):
            there = (chunk + i) % NZ
            arrive(half(wg_ref.at[there], j, zl), ("wy", i, j))
            if j < 2:
                pass_on(i, j)
            store(half(wg_ref.at[there], j, zl), half(wg_hbm.at[there], j, zl))
    for j in range(2):
        for i in (0, 1, 7, 2 if j % 2 else 6):
            there = (chunk + i) % NZ
            arrive(wg_ref.at[there, j, 1 - zl], ("wf", i, j))
            store(wg_ref.at[there, j, 1 - zl], wg_hbm.at[there, j, 1 - zl])
    for copy in stored:
        copy.wait()
    for copy in sent:
        copy.wait_send()
    for there, copy in planes:
        if there is None:
            copy.wait_send()
        else:
            pl.when(there)(copy.wait_send)
    assert len(sent) <= NSEM and len(ids) <= NSEM


def move_kernel(hg, wg, eg, hg_out, wg_out, eg_out, hg_v, wg_v, eg_v, isem, osem):
    moves = [(wg.at[i], wg_v.at[i], wg_out.at[i]) for i in range(NZ)]
    moves += [(eg, eg_v, eg_out), (hg, hg_v, hg_out)]
    loads = [pltpu.make_async_copy(a, b, isem.at[i]) for i, (a, b, _) in enumerate(moves)]
    stores = [pltpu.make_async_copy(b, c, osem.at[i]) for i, (_, b, c) in enumerate(moves)]
    for copy in loads:
        copy.start()
    for load, save in zip(loads, stores):
        load.wait()
        save.start()
    for copy in stores:
        copy.wait()


def move_results(*results):
    anywhere = [pl.BlockSpec(memory_space=pl.ANY)] * 3
    return pl.pallas_call(
        move_kernel,
        out_shape=[jax.ShapeDtypeStruct(r.shape, r.dtype) for r in results],
        in_specs=anywhere,
        out_specs=anywhere,
        scratch_shapes=[
            *[pltpu.VMEM(r.shape, r.dtype) for r in results],
            pltpu.SemaphoreType.DMA((NZ + 2,)),
            pltpu.SemaphoreType.DMA((NZ + 2,)),
        ],
        compiler_params=pltpu.CompilerParams(vmem_limit_bytes=62 * 2**20),
    )(*results)


def shards(hidden, proj_weight, task_embed, event_piece, censored, offset):
    rows = hidden.shape[0]
    scale = 1.0 / math.sqrt(rows * lax.axis_size("dp"))
    tasks, rank = task_embed.shape
    features, cols = proj_weight.shape
    hbm = pl.BlockSpec(memory_space=pl.ANY)

    def reduce_buffers():
        return [
            pltpu.VMEM((NZ, 2, NX, B, B), BF),
            pltpu.VMEM((NZ, NX, B, B), BF),
            pltpu.VMEM((NZ, NX, B, B), BF),
            pltpu.VMEM((NZ, NX, B, B), BF),
            pltpu.VMEM((NZ, B, B), BF),
            pltpu.VMEM((NZ, B, B), BF),
        ]

    hidden_grad, weight_grad, embed_grad = pl.pallas_call(
        functools.partial(kernel, scale),
        out_shape=(
            jax.ShapeDtypeStruct((B, rows), BF),
            jax.ShapeDtypeStruct((NZ, NX, 2, B, cols), BF),
            jax.ShapeDtypeStruct((NY, tasks // NY, rank), BF),
        ),
        in_specs=[hbm] * 6,
        out_specs=(hbm, hbm, hbm),
        scratch_shapes=[
            pltpu.VMEM((features, cols), BF),
            pltpu.VMEM((tasks, rank), BF),
            pltpu.VMEM((tasks, rows), jnp.int32),
            pltpu.VMEM((tasks, rows), jnp.int32),
            pltpu.VMEM((tasks, rows), jnp.int32),
            pltpu.VMEM((rank, tasks), BF),
            pltpu.VMEM((NZ, NX, 2, B, B), BF),
            pltpu.VMEM((NZ, NX, 2, B, B), BF),
            pltpu.VMEM((8, tasks, rows), BF),
            pltpu.VMEM((NY, NX, 2, B, B), BF),
            pltpu.VMEM((NZ, NX, B, B), BF),
            *reduce_buffers(),
            *reduce_buffers(),
            pltpu.VMEM((B, B), BF),
            pltpu.VMEM((NY, B, B), BF),
            pltpu.VMEM((NX, 2, B, B), BF),
            pltpu.VMEM((NX, 2, B, B), BF),
            pltpu.VMEM((NY, tasks // NY, rank), BF),
            pltpu.VMEM((NY, tasks // NY, rank), BF),
            pltpu.VMEM((tasks // NY, rank), BF),
            pltpu.VMEM((tasks // NY, rank), BF),
            pltpu.VMEM((B, rows), BF),
            pltpu.VMEM((NZ, NX, 2, B, cols), BF),
            pltpu.VMEM((NY, tasks // NY, rank), BF),
            pltpu.SemaphoreType.DMA((6,)),
            pltpu.SemaphoreType.DMA((32,)),
            pltpu.SemaphoreType.DMA((NZ, 2)),
            pltpu.SemaphoreType.DMA((NY,)),
            pltpu.SemaphoreType.DMA((NSEM,)),
            pltpu.SemaphoreType.DMA((NSEM,)),
        ],
        compiler_params=pltpu.CompilerParams(
            collective_id=0, has_side_effects=True, vmem_limit_bytes=62 * 2**20
        ),
    )(hidden, proj_weight, task_embed, event_piece, censored, offset)
    hidden_grad, weight_grad, embed_grad = move_results(hidden_grad, weight_grad, embed_grad)
    return (
        hidden_grad,
        weight_grad.reshape(features, cols),
        embed_grad.reshape(tasks, rank),
    )


def solution(mesh):
    return jax.shard_map(
        shards,
        mesh=mesh,
        in_specs=(
            P("dp", "task"),
            P(None, "task"),
            P("task", None),
            P("task", "dp"),
            P("task", "dp"),
            P("task", "dp"),
        ),
        out_specs=(P("task", "dp"), P(None, "task"), P("task", None)),
        check_vma=False,
    )
```
